32 devices in a mesh: dp: 8 (over z, y), mp: 4 (over x, core).
Axes of the slice: x: 2, y: 2, z: 4, core: 2. Of those that a mesh axis runs over, the one named last changes fastest.
Arguments:
- latents: bfloat16 [5120, 1280], P('dp', 'mp'), may hold values from -8 to 8
- time_embed: bfloat16 [20, 1280], replicated, may hold values from -6 to 6
- text_states: bfloat16 [8, 77, 2048], replicated, may hold values from -6 to 6
- item_prompt: int32 [20], replicated, may hold values from 0 to 7
- prompt_length: int32 [8], replicated, may hold values from 1 to 77
- out_grad: bfloat16 [5120, 1280], P('dp', 'mp'), may hold values from -6 to 6
- resnorm_gain_a: float32 [1280], P('mp'), may hold values from 0.5 to 1.5
- resnorm_bias_a: float32 [1280], P('mp'), may hold values from -1.8 to 1.8
- conv_weight_a: bfloat16 [9, 1280, 1280], P(None, 'dp', 'mp'), may hold values from -0.0546875 to 0.0546875
- conv_bias_a: float32 [1280], P('mp'), may hold values from -1.8 to 1.8
- time_weight: bfloat16 [1280, 1280], P('dp', 'mp'), may hold values from -0.15625 to 0.15625
- time_bias: float32 [1280], P('mp'), may hold values from -1.8 to 1.8
- resnorm_gain_b: float32 [1280], P('mp'), may hold values from 0.5 to 1.5
- resnorm_bias_b: float32 [1280], P('mp'), may hold values from -1.8 to 1.8
- conv_weight_b: bfloat16 [9, 1280, 1280], P(None, 'dp', 'mp'), may hold values from -0.078125 to 0.078125
- conv_bias_b: float32 [1280], P('mp'), may hold values from -1.8 to 1.8
- attn_norm_gain: float32 [1280], P('mp'), may hold values from 0.5 to 1.5
- attn_norm_bias: float32 [1280], P('mp'), may hold values from -1.8 to 1.8
- qkv_weight: bfloat16 [3, 1280, 1280], P(None, 'dp', 'mp'), may hold values from -0.15625 to 0.15625
- attn_out_weight: bfloat16 [1280, 1280], P('mp', 'dp'), may hold values from -0.5 to 0.5
- attn_out_bias: float32 [1280], P('mp'), may hold values from -1.8 to 1.8
- cross_norm_gain: float32 [1280], P('mp'), may hold values from 0.5 to 1.5
- cross_norm_bias: float32 [1280], P('mp'), may hold values from -1.8 to 1.8
- cross_query_weight: bfloat16 [1280, 1280], P('dp', 'mp'), may hold values from -0.15625 to 0.15625
- cross_kv_weight: bfloat16 [2, 2048, 1280], P(None, 'dp', 'mp'), may hold values from -0.125 to 0.125
- cross_out_weight: bfloat16 [1280, 1280], P('mp', 'dp'), may hold values from -0.5 to 0.5
- cross_out_bias: float32 [1280], P('mp'), may hold values from -1.8 to 1.8
- geglu_norm_gain: float32 [1280], P('mp'), may hold values from 0.5 to 1.5
- geglu_norm_bias: float32 [1280], P('mp'), may hold values from -1.8 to 1.8
- geglu_in_weight: bfloat16 [1280, 2, 5120], P('dp', None, 'mp'), may hold values from -0.15625 to 0.15625
- geglu_in_bias: float32 [2, 5120], P(None, 'mp'), may hold values from -1.8 to 1.8
- geglu_out_weight: bfloat16 [5120, 1280], P('mp', 'dp'), may hold values from -0.078125 to 0.078125
- geglu_out_bias: float32 [1280], P('mp'), may hold values from -1.8 to 1.8
Outputs:
- block_out: bfloat16 [5120, 1280], P('dp', 'mp')
- latents_grad: float32 [5120, 1280], P('dp', 'mp')
- resnorm_gain_a_grad: float32 [1280], P('mp')
- resnorm_bias_a_grad: float32 [1280], P('mp')
- conv_weight_a_grad: float32 [9, 1280, 1280], P(None, 'dp', 'mp')
- conv_bias_a_grad: float32 [1280], P('mp')
- time_weight_grad: float32 [1280, 1280], P('dp', 'mp')
- time_bias_grad: float32 [1280], P('mp')
- resnorm_gain_b_grad: float32 [1280], P('mp')
- resnorm_bias_b_grad: float32 [1280], P('mp')
- conv_weight_b_grad: float32 [9, 1280, 1280], P(None, 'dp', 'mp')
- conv_bias_b_grad: float32 [1280], P('mp')
- attn_norm_gain_grad: float32 [1280], P('mp')
- attn_norm_bias_grad: float32 [1280], P('mp')
- qkv_weight_grad: float32 [3, 1280, 1280], P(None, 'dp', 'mp')
- attn_out_weight_grad: float32 [1280, 1280], P('mp', 'dp')
- attn_out_bias_grad: float32 [1280], P('mp')
- cross_norm_gain_grad: float32 [1280], P('mp')
- cross_norm_bias_grad: float32 [1280], P('mp')
- cross_query_weight_grad: float32 [1280, 1280], P('dp', 'mp')
- cross_kv_weight_grad: float32 [2, 2048, 1280], P(None, 'dp', 'mp')
- cross_out_weight_grad: float32 [1280, 1280], P('mp', 'dp')
- cross_out_bias_grad: float32 [1280], P('mp')
- geglu_norm_gain_grad: float32 [1280], P('mp')
- geglu_norm_bias_grad: float32 [1280], P('mp')
- geglu_in_weight_grad: float32 [1280, 2, 5120], P('dp', None, 'mp')
- geglu_in_bias_grad: float32 [2, 5120], P(None, 'mp')
- geglu_out_weight_grad: float32 [5120, 1280], P('mp', 'dp')
- geglu_out_bias_grad: float32 [1280], P('mp')
The draws below stay inside these ranges and needn't reach their ends.
All inputs are finite; a program needn't handle non-finite values.
Results may differ from the reference program's by a relative error of at most 0.03.
Values may be sent and summed in bfloat16 or wider, within the bound.
No kernel may reach another device: no remote copies, remote signals or barrier semaphores. Data moves between devices by JAX's collectives and lax.ppermute only.
A program may use at most 384 MiB of HBM per device.

```python
import math
import jax
import jax.numpy as jnp
from jax import lax

C = 1280
GROUPS = 32
HEAD = 64
FF = 5120
TXT = 2048
TEMB = 1280
TXT_LEN = 77
IMG_H = 16
IMG_W = 16
PROMPTS = 8
TOKENS = 5120
ITEMS = 20


def draw_latents(key, part):
    subkeys = jax.random.split(key, 4)
    pixels = IMG_H * IMG_W
    item_count = TOKENS // pixels
    base_draw = jnp.clip(jax.random.normal(subkeys[0], (TOKENS, C), jnp.float32), -4.0, 4.0)
    ramp_factor = 0.6 + 1.2 * jnp.arange(item_count, dtype=jnp.float32) / item_count
    item_scale = jnp.exp(jax.random.uniform(subkeys[1], (item_count,), jnp.float32, math.log(0.5), math.log(1.0))) * ramp_factor
    row_scale = jnp.exp(jax.random.uniform(subkeys[2], (TOKENS,), jnp.float32, math.log(0.6), math.log(1.7)))
    chan_scale = jnp.exp(jax.random.uniform(subkeys[3], (C,), jnp.float32, math.log(0.6), math.log(1.7)))
    scaled = base_draw * (jnp.repeat(item_scale, pixels) * row_scale)[:, None] * chan_scale[None, :]
    return jnp.clip(scaled, -8.0, 8.0).astype(jnp.bfloat16)


def place_ends(array, key, low, high):
    shape = array.shape
    place = [jax.random.randint(jax.random.fold_in(key, axis), (), 0, shape[axis]) for axis in range(len(shape))]
    array = array.at[tuple(place)].set(low)
    longest = shape.index(max(shape))
    place[longest] = (place[longest] + 1) % shape[longest]
    return array.at[tuple(place)].set(high)


def block_scale(own_key, dims, cuts, least, largest):
    factor_of, own = 1.0, jax.random.fold_in(own_key, 6)
    for position, shards_of in cuts:
        steps = jnp.exp(jax.random.uniform(jax.random.fold_in(own, position), (shards_of,), jnp.float32, least / len(cuts), largest / len(cuts)))
        factor_of = factor_of * jnp.repeat(steps, dims[position] // shards_of).reshape([-1 if axis == position else 1 for axis in range(len(dims))])
    return factor_of


def centred(own_key, extent, width, bound, shards=(), kind=jnp.bfloat16):
    level = block_scale(own_key, extent, shards, -0.22, 0.18) if shards else 1.0
    array = jax.random.normal(own_key, extent, jnp.float32) * width * level
    return jnp.minimum(jnp.maximum(array, -bound), bound).astype(kind)


def setup_inputs(seed: int = 0) -> dict:
    key_list = jax.random.split(jax.random.key(seed), 34)
    return {
        "latents": draw_latents(jax.random.fold_in(key_list[33], 71), 0),
        "time_embed": centred(key_list[1], (ITEMS, TEMB), 1.0, 6.0),
        "text_states": centred(key_list[2], (PROMPTS, TXT_LEN, TXT), 1.0, 6.0),
        "item_prompt": place_ends(jax.random.randint(key_list[3], (ITEMS,), 0, PROMPTS), jax.random.fold_in(key_list[3], 1), 0, PROMPTS - 1).astype(jnp.int32),
        "prompt_length": place_ends(jax.random.randint(key_list[4], (PROMPTS,), 1, TXT_LEN + 1), jax.random.fold_in(key_list[4], 1), 1, TXT_LEN).astype(jnp.int32),
        "out_grad": centred(key_list[5], (TOKENS, C), 1.0, 6.0, ((0, 8), (1, 4))),
        "resnorm_gain_a": jnp.clip(1.0 + 0.1 * jax.random.normal(key_list[6], (C,), jnp.float32), 0.5, 1.5),
        "resnorm_bias_a": centred(key_list[7], (C,), 0.3, 1.8, ((0, 4),), jnp.float32),
        "conv_weight_a": centred(key_list[8], (9, C, C), (9 * C) ** -0.5, 0.0546875, ((1, 8), (2, 4))),
        "conv_bias_a": centred(key_list[9], (C,), 0.3, 1.8, ((0, 4),), jnp.float32),
        "time_weight": centred(key_list[10], (TEMB, C), TEMB ** -0.5, 0.15625, ((0, 8), (1, 4))),
        "time_bias": centred(key_list[11], (C,), 0.3, 1.8, ((0, 4),), jnp.float32),
        "resnorm_gain_b": jnp.clip(1.0 + 0.1 * jax.random.normal(key_list[12], (C,), jnp.float32), 0.5, 1.5),
        "resnorm_bias_b": centred(key_list[13], (C,), 0.3, 1.8, ((0, 4),), jnp.float32),
        "conv_weight_b": centred(key_list[14], (9, C, C), (9 * C // 2) ** -0.5, 0.078125, ((1, 8), (2, 4))),
        "conv_bias_b": centred(key_list[15], (C,), 0.3, 1.8, ((0, 4),), jnp.float32),
        "attn_norm_gain": jnp.clip(1.0 + 0.1 * jax.random.normal(key_list[16], (C,), jnp.float32), 0.5, 1.5),
        "attn_norm_bias": centred(key_list[17], (C,), 0.3, 1.8, ((0, 4),), jnp.float32),
        "qkv_weight": centred(key_list[18], (3, C, C), C ** -0.5, 0.15625, ((1, 8), (2, 4))),
        "attn_out_weight": centred(key_list[19], (C, C), (C // 8) ** -0.5, 0.5, ((0, 4), (1, 8))),
        "attn_out_bias": centred(key_list[20], (C,), 0.3, 1.8, ((0, 4),), jnp.float32),
        "cross_norm_gain": jnp.clip(1.0 + 0.1 * jax.random.normal(key_list[21], (C,), jnp.float32), 0.5, 1.5),
        "cross_norm_bias": centred(key_list[22], (C,), 0.3, 1.8, ((0, 4),), jnp.float32),
        "cross_query_weight": centred(key_list[23], (C, C), C ** -0.5, 0.15625, ((0, 8), (1, 4))),
        "cross_kv_weight": centred(key_list[24], (2, TXT, C), TXT ** -0.5, 0.125, ((1, 8), (2, 4))),
        "cross_out_weight": centred(key_list[25], (C, C), (C // 8) ** -0.5, 0.5, ((0, 4), (1, 8))),
        "cross_out_bias": centred(key_list[26], (C,), 0.3, 1.8, ((0, 4),), jnp.float32),
        "geglu_norm_gain": jnp.clip(1.0 + 0.1 * jax.random.normal(key_list[27], (C,), jnp.float32), 0.5, 1.5),
        "geglu_norm_bias": centred(key_list[28], (C,), 0.3, 1.8, ((0, 4),), jnp.float32),
        "geglu_in_weight": centred(key_list[29], (C, 2, FF), C ** -0.5, 0.15625, ((0, 8), (2, 4))),
        "geglu_in_bias": centred(key_list[30], (2, FF), 0.3, 1.8, ((1, 4),), jnp.float32),
        "geglu_out_weight": centred(key_list[31], (FF, C), FF ** -0.5, 0.078125, ((0, 4), (1, 8))),
        "geglu_out_bias": centred(key_list[32], (C,), 0.3, 1.8, ((0, 4),), jnp.float32),
    }


EPS = 1e-05
HIGH = lax.Precision.HIGHEST
NEG = -1e+30

@jax.custom_vjp
def low(v):
    return lax.optimization_barrier(v.astype(jnp.bfloat16)).astype(jnp.float32)

@jax.custom_vjp
def low_back(v):
    return v

def low_keep(v):
    return (low(v), None)

def low_pass(kept, grad):
    return (grad,)

def back_keep(v):
    return (v, None)

def back_low(kept, grad):
    return (low(grad),)
low.defvjp(low_keep, low_pass)
low_back.defvjp(back_keep, back_low)

def matmul_hi(operand_a, operand_b):
    return jnp.matmul(operand_a, operand_b, precision=HIGH)

def round_both(array_in):
    return low(low_back(array_in))

def group_norm(array_in, gain, shift):
    count, pixels, chans = array_in.shape
    grouped = array_in.reshape(count, pixels, GROUPS, chans // GROUPS)
    mean_value = lax.optimization_barrier(jnp.mean(grouped, axis=(1, 3), keepdims=True))
    square = lax.optimization_barrier(jnp.mean(grouped * grouped, axis=(1, 3), keepdims=True))
    scaled = (grouped - mean_value) * lax.rsqrt(square - mean_value * mean_value + EPS)
    return scaled.reshape(count, pixels, chans) * gain + shift

def layer_norm(array_in, gain, shift):
    mean_value = lax.optimization_barrier(jnp.mean(array_in, axis=-1, keepdims=True))
    square = lax.optimization_barrier(jnp.mean(array_in * array_in, axis=-1, keepdims=True))
    return (array_in - mean_value) * lax.rsqrt(square - mean_value * mean_value + EPS) * gain + shift

def conv_image(array_in, weight):
    count = array_in.shape[0]
    image = array_in.reshape(count, IMG_H, IMG_W, array_in.shape[-1])
    padded = jnp.pad(image, ((0, 0), (1, 1), (1, 1), (0, 0)))
    total = jnp.zeros((count, IMG_H, IMG_W, weight.shape[-1]), jnp.float32)
    for tap_index in range(9):
        row_start = tap_index // 3
        col_start = tap_index % 3
        window = padded[:, row_start:row_start + IMG_H, col_start:col_start + IMG_W, :]
        total = total + matmul_hi(window, weight[tap_index])
    return total.reshape(count, IMG_H * IMG_W, weight.shape[-1])

def attention(query, key_rows, value_rows, live):
    count, length, chans = query.shape
    heads = chans // HEAD
    score_scale = 1.0 / math.sqrt(HEAD)
    query_heads = query.reshape(count, length, heads, HEAD)
    key_heads = key_rows.reshape(count, key_rows.shape[1], heads, HEAD)
    value_heads = value_rows.reshape(count, value_rows.shape[1], heads, HEAD)
    scores = low_back(jnp.einsum('nqhd,nkhd->nhqk', query_heads, key_heads, precision=HIGH) * score_scale)
    if live is not None:
        scores = jnp.where(live[:, None, None, :] > 0.5, scores, NEG)
    attn_probs = low(jax.nn.softmax(scores, axis=-1))
    result = jnp.einsum('nhqk,nkhd->nqhd', attn_probs, value_heads, precision=HIGH)
    return result.reshape(count, length, chans)

def reference(latents, time_embed, text_states, item_prompt, prompt_length, out_grad, resnorm_gain_a, resnorm_bias_a, conv_weight_a, conv_bias_a, time_weight, time_bias, resnorm_gain_b, resnorm_bias_b, conv_weight_b, conv_bias_b, attn_norm_gain, attn_norm_bias, qkv_weight, attn_out_weight, attn_out_bias, cross_norm_gain, cross_norm_bias, cross_query_weight, cross_kv_weight, cross_out_weight, cross_out_bias, geglu_norm_gain, geglu_norm_bias, geglu_in_weight, geglu_in_bias, geglu_out_weight, geglu_out_bias):
    params = tuple((weight.astype(jnp.float32) for weight in (resnorm_gain_a, resnorm_bias_a, conv_weight_a, conv_bias_a, time_weight, time_bias, resnorm_gain_b, resnorm_bias_b, conv_weight_b, conv_bias_b, attn_norm_gain, attn_norm_bias, qkv_weight, attn_out_weight, attn_out_bias, cross_norm_gain, cross_norm_bias, cross_query_weight, cross_kv_weight, cross_out_weight, cross_out_bias, geglu_norm_gain, geglu_norm_bias, geglu_in_weight, geglu_in_bias, geglu_out_weight, geglu_out_bias)))
    pixels = IMG_H * IMG_W
    offset = pixels // 4
    group_size = math.gcd(ITEMS, max(1, 4096 // pixels))
    group_count = ITEMS // group_size
    time_in = low(jax.nn.silu(time_embed.astype(jnp.float32)))
    text_in = text_states.astype(jnp.float32)
    item_live = (jnp.arange(TXT_LEN, dtype=jnp.int32)[None, :] < jnp.take(prompt_length, item_prompt)[:, None]).astype(jnp.float32)

    def forward(latent_in, weights):
        resnorm_gain_a, resnorm_bias_a, conv_weight_a, conv_bias_a, time_weight, time_bias, resnorm_gain_b, resnorm_bias_b, conv_weight_b, conv_bias_b, attn_norm_gain, attn_norm_bias, qkv_weight, attn_out_weight, attn_out_bias, cross_norm_gain, cross_norm_bias, cross_query_weight, cross_kv_weight, cross_out_weight, cross_out_bias, geglu_norm_gain, geglu_norm_bias, geglu_in_weight, geglu_in_bias, geglu_out_weight, geglu_out_bias = weights
        time_terms = low_back(matmul_hi(time_in, time_weight)) + time_bias
        text_keys = round_both(matmul_hi(text_in, cross_kv_weight[0]))
        text_values = round_both(matmul_hi(text_in, cross_kv_weight[1]))
        item_keys = jnp.take(text_keys, item_prompt, axis=0)
        item_values = jnp.take(text_values, item_prompt, axis=0)
        packed = jnp.roll(latent_in, offset, axis=0)

        def one_group(pieces):
            latent_block, term_rows, group_keys, group_values, group_live = pieces
            act_a = low(jax.nn.silu(group_norm(latent_block, resnorm_gain_a, resnorm_bias_a)))
            middle = low_back(conv_image(act_a, conv_weight_a)) + conv_bias_a + term_rows[:, None, :]
            act_b = low(jax.nn.silu(group_norm(middle, resnorm_gain_b, resnorm_bias_b)))
            resid = latent_block + low_back(conv_image(act_b, conv_weight_b)) + conv_bias_b
            norm_one = low(layer_norm(resid, attn_norm_gain, attn_norm_bias))
            query = round_both(matmul_hi(norm_one, qkv_weight[0]))
            key_rows = round_both(matmul_hi(norm_one, qkv_weight[1]))
            value_rows = round_both(matmul_hi(norm_one, qkv_weight[2]))
            attended = round_both(attention(query, key_rows, value_rows, None))
            resid_two = resid + low_back(matmul_hi(attended, attn_out_weight)) + attn_out_bias
            norm_two = low(layer_norm(resid_two, cross_norm_gain, cross_norm_bias))
            cross_query = round_both(matmul_hi(norm_two, cross_query_weight))
            cross_attended = round_both(attention(cross_query, group_keys, group_values, group_live))
            resid_three = resid_two + low_back(matmul_hi(cross_attended, cross_out_weight)) + cross_out_bias
            norm_three = low(layer_norm(resid_three, geglu_norm_gain, geglu_norm_bias))
            pre_ff = low_back(matmul_hi(norm_three, geglu_in_weight.reshape(C, 2 * FF)))
            pre_ff = pre_ff.reshape(group_size, pixels, 2, FF) + geglu_in_bias
            hidden = low(pre_ff[:, :, 0] * jax.nn.gelu(pre_ff[:, :, 1], approximate=False))
            return resid_three + low_back(matmul_hi(hidden, geglu_out_weight)) + geglu_out_bias
        outputs = lax.map(jax.checkpoint(one_group), (packed.reshape(group_count, group_size, pixels, C), time_terms.reshape(group_count, group_size, C), item_keys.reshape(group_count, group_size, TXT_LEN, C), item_values.reshape(group_count, group_size, TXT_LEN, C), item_live.reshape(group_count, group_size, TXT_LEN)))
        return jnp.roll(outputs.reshape(TOKENS, C), -offset, axis=0)
    primal, pullback = jax.vjp(forward, latents.astype(jnp.float32), params)
    latent_grad, weight_grads = pullback(out_grad.astype(jnp.float32))
    return (primal.astype(jnp.bfloat16), latent_grad, weight_grads[0], weight_grads[1], weight_grads[2], weight_grads[3], weight_grads[4], weight_grads[5], weight_grads[6], weight_grads[7], weight_grads[8], weight_grads[9], weight_grads[10], weight_grads[11], weight_grads[12], weight_grads[13], weight_grads[14], weight_grads[15], weight_grads[16], weight_grads[17], weight_grads[18], weight_grads[19], weight_grads[20], weight_grads[21], weight_grads[22], weight_grads[23], weight_grads[24], weight_grads[25], weight_grads[26])
```

```python
import functools
import math

import jax
import jax.numpy as jnp
from jax import lax
from jax.experimental import pallas as pl
from jax.experimental.pallas import tpu as pltpu
from jax.sharding import Mesh
from jax.sharding import PartitionSpec as P

C = 1280
GROUPS = 32
HEAD = 64
TXT = 2048
TEMB = 1280
TXT_LEN = 77
TXT_PAD = 80
IMG_H = 16
IMG_W = 16
PIXELS = IMG_H * IMG_W
PROMPTS = 8


EPS = 1e-05
HIGH = lax.Precision.HIGHEST
NEG = -1e30
SCALE = 1.0 / math.sqrt(HEAD)
VMEM_LIMIT = 48 * 1024 * 1024


def narrow(array_in):
    return array_in.astype(jnp.bfloat16)


def wide(array_in):
    return array_in.astype(jnp.float32)


def product(operand_a, operand_b):
    return jnp.dot(operand_a, operand_b, preferred_element_type=jnp.float32)


def inner_rows(operand_a, operand_b):
    return lax.dot_general(
        operand_a, operand_b, (((0,), (0,)), ((), ())), preferred_element_type=jnp.float32
    )


def outer_cols(operand_a, operand_b):
    return lax.dot_general(
        operand_a, operand_b, (((1,), (1,)), ((), ())), preferred_element_type=jnp.float32
    )


def silu_back(grad_in, pre_act):
    sigmoid_value = jax.nn.sigmoid(pre_act)
    return grad_in * sigmoid_value * (1.0 + pre_act * (1.0 - sigmoid_value))


def geglu(value_part, gate_part):
    return value_part * jax.nn.gelu(gate_part, approximate=False)


def head_cols(head_index):
    return slice(head_index * HEAD, (head_index + 1) * HEAD)


def softmax_rows(scores):
    top_score = jnp.max(scores, axis=1, keepdims=True)
    weights = jnp.exp(scores - top_score)
    return weights / jnp.sum(weights, axis=1, keepdims=True)


def unit_back(query, keys, values, probs, grad_rows):
    grad_probs = outer_cols(grad_rows, values)
    delta = jnp.sum(probs * grad_probs, axis=1, keepdims=True)
    grad_scores = narrow(probs * (grad_probs - delta))
    grad_query = product(grad_scores, keys) * SCALE
    grad_keys = inner_rows(grad_scores, query) * SCALE
    grad_values = inner_rows(narrow(probs), grad_rows)
    return grad_query, grad_keys, grad_values


def self_units(row_count):
    units = [slice(s, s + PIXELS) for s in range(0, row_count - PIXELS + 1, PIXELS)]
    return units, slice(len(units) * PIXELS, row_count)


def self_kernel(qkv_ref, far_ref, out_ref):
    row_count, width = out_ref.shape
    whole, part = self_units(row_count)
    for rows in whole + [part]:
        outs = []
        for head_index in range(width // HEAD):
            cols = head_cols(head_index)
            query, keys, values = qkv_ref[0, rows, cols], qkv_ref[1, rows, cols], qkv_ref[2, rows, cols]
            if rows == part:
                keys = jnp.concatenate([keys, far_ref[0, :, cols]], axis=0)
                values = jnp.concatenate([values, far_ref[1, :, cols]], axis=0)
            probs = softmax_rows(outer_cols(query, keys) * SCALE)
            outs.append(product(narrow(probs), values))
        out_ref[rows, :] = narrow(jnp.concatenate(outs, axis=1))


def self_back_kernel(qkv_ref, far_ref, grad_ref, dqkv_ref, dfar_ref):
    row_count, width = grad_ref.shape
    whole, part = self_units(row_count)
    near = part.stop - part.start
    for rows in whole + [part]:
        parts = ([], [], [])
        for head_index in range(width // HEAD):
            cols = head_cols(head_index)
            query, keys, values = qkv_ref[0, rows, cols], qkv_ref[1, rows, cols], qkv_ref[2, rows, cols]
            if rows == part:
                keys = jnp.concatenate([keys, far_ref[0, :, cols]], axis=0)
                values = jnp.concatenate([values, far_ref[1, :, cols]], axis=0)
            probs = softmax_rows(outer_cols(query, keys) * SCALE)
            for kept, grad in zip(parts, unit_back(query, keys, values, probs, grad_ref[rows, cols])):
                kept.append(grad)
        grads = [jnp.concatenate(kept, axis=1) for kept in parts]
        dqkv_ref[0, rows, :] = narrow(grads[0])
        for index in (1, 2):
            if rows == part:
                dqkv_ref[index, rows, :] = narrow(grads[index][:near])
                dfar_ref[index - 1, :, :] = narrow(grads[index][near:])
            else:
                dqkv_ref[index, rows, :] = narrow(grads[index])


def cross_probs(query, keys, length):
    scores = outer_cols(query, keys) * SCALE
    live = lax.broadcasted_iota(jnp.int32, scores.shape, 1) < length
    return softmax_rows(jnp.where(live, scores, NEG))


def cross_kernel(prompt_ref, length_ref, query_ref, text_ref, out_ref):
    row_count, width = out_ref.shape
    whole, part = self_units(row_count)
    for slot, rows in enumerate(whole + [part]):
        prompt, length = prompt_ref[slot], length_ref[slot]
        keys, values = text_ref[0, prompt], text_ref[1, prompt]
        outs = []
        for head_index in range(width // HEAD):
            cols = head_cols(head_index)
            probs = cross_probs(query_ref[rows, cols], keys[:, cols], length)
            outs.append(product(narrow(probs), values[:, cols]))
        out_ref[rows, :] = narrow(jnp.concatenate(outs, axis=1))


def cross_back_kernel(prompt_ref, length_ref, query_ref, text_ref, grad_ref, dquery_ref, dtext_ref):
    row_count, width = grad_ref.shape
    whole, part = self_units(row_count)
    dtext_ref[...] = jnp.zeros_like(dtext_ref)
    for slot, rows in enumerate(whole + [part]):
        prompt, length = prompt_ref[slot], length_ref[slot]
        keys, values = text_ref[0, prompt], text_ref[1, prompt]
        parts = ([], [], [])
        for head_index in range(width // HEAD):
            cols = head_cols(head_index)
            query = query_ref[rows, cols]
            probs = cross_probs(query, keys[:, cols], length)
            for kept, grad in zip(
                parts, unit_back(query, keys[:, cols], values[:, cols], probs, grad_ref[rows, cols])
            ):
                kept.append(grad)
        grads = [jnp.concatenate(kept, axis=1) for kept in parts]
        dquery_ref[rows, :] = narrow(grads[0])
        dtext_ref[0, prompt] += grads[1]
        dtext_ref[1, prompt] += grads[2]


def in_vmem():
    return pl.BlockSpec(memory_space=pltpu.VMEM)


def in_smem():
    return pl.BlockSpec(memory_space=pltpu.SMEM)


def kernel_call(kernel, specs, outs, flops, *operands):
    shapes = [jax.ShapeDtypeStruct(shape, dtype) for shape, dtype in outs]
    moved = sum(o.size * o.dtype.itemsize for o in operands) + sum(
        math.prod(shape) * jnp.dtype(dtype).itemsize for shape, dtype in outs
    )
    results = pl.pallas_call(
        kernel,
        out_shape=shapes,
        in_specs=specs,
        out_specs=[in_vmem() for _ in shapes],
        compiler_params=pltpu.CompilerParams(vmem_limit_bytes=VMEM_LIMIT),
        cost_estimate=pl.CostEstimate(flops=flops, bytes_accessed=moved, transcendentals=flops // 128),
    )(*operands)
    return results[0] if len(results) == 1 else results


PAIR = ((0, 1), (1, 0))


def swap(array_in, axis):
    return lax.ppermute(array_in, axis, PAIR)


def pick(array_in, index, axis):
    return lax.dynamic_index_in_dim(array_in, index, axis, keepdims=False)


def owner_order(pieces):
    at_x, at_c = lax.axis_index("x") == 0, lax.axis_index("c") == 0
    half = [jnp.where(at_c, pieces[s], pieces[s ^ 1]) for s in range(4)]
    return [jnp.where(at_x, half[s], half[s ^ 2]) for s in range(4)]


def gather_mp(array_in):
    far = swap(array_in, "x")
    return owner_order([array_in, swap(array_in, "c"), far, swap(far, "c")])


def scatter_sum_mp(stacked):
    at_x, at_c = lax.axis_index("x"), lax.axis_index("c")
    kept = wide(pick(stacked, at_c, 1))
    got = wide(swap(pick(stacked, 1 - at_c, 1), "c"))
    total = kept + got
    return pick(total, at_x, 0) + wide(swap(narrow(pick(total, 1 - at_x, 0)), "x"))


def gather_eight(array_in):
    middle = array_in.shape[0] // 2
    by_h, by_x = swap(array_in, "h"), swap(array_in, "x")
    across = jnp.concatenate([swap(by_h[:middle], "x"), swap(by_x[middle:], "h")], axis=0)
    near = [array_in, by_x, by_h, across]
    far = [swap(piece, "c") for piece in near]
    at_c, at_h = lax.axis_index("c") == 0, lax.axis_index("h") == 0
    at_x = lax.axis_index("x") == 0
    half = [[jnp.where(at_c, n, f), jnp.where(at_c, f, n)] for n, f in zip(near, far)]
    quarter = [
        [jnp.where(at_x, half[s][c], half[s ^ 1][c]) for c in range(2)] for s in range(4)
    ]
    return [jnp.where(at_h, quarter[s][c], quarter[s ^ 2][c]) for s in range(4) for c in range(2)]


def scatter_sum_eight(stacked):
    at_h, at_x, at_c = lax.axis_index("h"), lax.axis_index("x"), lax.axis_index("c")
    total = wide(pick(stacked, at_c, 2)) + wide(swap(pick(stacked, 1 - at_c, 2), "c"))
    middle = total.shape[2] // 2
    upper, lower = total[:, :, :middle], total[:, :, middle:]
    upper = pick(upper, at_x, 1) + wide(swap(narrow(pick(upper, 1 - at_x, 1)), "x"))
    lower = pick(lower, at_h, 0) + wide(swap(narrow(pick(lower, 1 - at_h, 0)), "h"))
    upper = pick(upper, at_h, 0) + wide(swap(narrow(pick(upper, 1 - at_h, 0)), "h"))
    lower = pick(lower, at_x, 0) + wide(swap(narrow(pick(lower, 1 - at_x, 0)), "x"))
    return jnp.concatenate([upper, lower], axis=0)


def exchange_mp(stacked):
    place = 2 * lax.axis_index("x") + lax.axis_index("c")
    pieces = [pick(stacked, place ^ s, 0) for s in range(4)]
    far = swap(pieces[3], "c")
    return owner_order([pieces[0], swap(pieces[1], "c"), swap(pieces[2], "x"), swap(far, "x")])


def join_h(array_in, axis):
    other = swap(array_in, "h")
    first = lax.axis_index("h") == 0
    return jnp.concatenate(
        [jnp.where(first, array_in, other), jnp.where(first, other, array_in)], axis=axis
    )


def sum_g(array_in):
    size = lax.axis_size("g")
    total = array_in
    for step in range(1, size):
        total = total + rotate_g(array_in, step)
    return total


def gather_h(array_in, axis):
    other = swap(array_in, "h")
    first = lax.axis_index("h") == 0
    return jnp.stack(
        [jnp.where(first, array_in, other), jnp.where(first, other, array_in)], axis=axis
    )


def scatter_sum_h(array_in, axis):
    at_h = lax.axis_index("h")
    sent = narrow(pick(array_in, 1 - at_h, axis))
    return wide(pick(array_in, at_h, axis)) + wide(swap(sent, "h"))


def rotate_g(array_in, step):
    size = lax.axis_size("g")
    return lax.ppermute(array_in, "g", [(i, (i + step) % size) for i in range(size)])


def sum_pixels(array_in):
    size, at_g = lax.axis_size("g"), lax.axis_index("g")
    count, rows, width = array_in.shape
    share = scatter_sum_h(array_in.reshape(count, 2, rows // 2, width), 1)
    blocks = narrow(share).reshape(count, size, rows // 2 // size, width)
    total = pick(share.reshape(blocks.shape), at_g, 1)
    for step in range(1, size):
        total = total + wide(rotate_g(pick(blocks, (at_g + step) % size, 1), step))
    total = narrow(total)
    held = jnp.zeros_like(blocks)
    held = lax.dynamic_update_index_in_dim(held, total, at_g, 1)
    for step in range(1, size):
        got = rotate_g(total, step)
        held = lax.dynamic_update_index_in_dim(held, got, (at_g + size - step) % size, 1)
    return gather_h(held.reshape(count, rows // 2, width), 1).reshape(array_in.shape)


def shift_rows(array_in, to_next, count):
    size = lax.axis_size("g") * lax.axis_size("h")
    pairs = [(i, (i + 1) % size) for i in range(size)]
    if to_next:
        edge = lax.ppermute(array_in[-count:], ("g", "h"), pairs)
        return jnp.concatenate([edge, array_in[:-count]], axis=0)
    edge = lax.ppermute(array_in[:count], ("g", "h"), [(j, i) for i, j in pairs])
    return jnp.concatenate([array_in[count:], edge], axis=0)


def turn(array_in, count, forward):
    moved = jnp.roll(array_in, -count if forward else count, axis=0)
    return jnp.where(lax.axis_index("h") == 0, array_in, moved)


def conv_apply(act, weight):
    images = act.reshape(-1, IMG_H, IMG_W, act.shape[1])
    result = lax.conv_general_dilated(
        images,
        weight.reshape(3, 3, *weight.shape[1:]),
        (1, 1),
        ((1, 1), (1, 1)),
        dimension_numbers=("NHWC", "HWIO", "NHWC"),
        preferred_element_type=jnp.float32,
    )
    return result.reshape(act.shape[0], weight.shape[2])


def conv_back_input(grad, weight):
    images = grad.reshape(-1, IMG_H, IMG_W, grad.shape[1])
    result = lax.conv_general_dilated(
        images,
        weight.reshape(3, 3, *weight.shape[1:])[::-1, ::-1],
        (1, 1),
        ((1, 1), (1, 1)),
        dimension_numbers=("NHWC", "HWOI", "NHWC"),
        preferred_element_type=jnp.float32,
    )
    return result.reshape(grad.shape[0], weight.shape[1])


def conv_back_weight(act, grad):
    result = lax.conv_general_dilated(
        act.reshape(-1, IMG_H, IMG_W, act.shape[1]),
        grad.reshape(-1, IMG_H, IMG_W, grad.shape[1]),
        (1, 1),
        ((1, 1), (1, 1)),
        dimension_numbers=("CHWN", "IHWO", "HWNC"),
        preferred_element_type=jnp.float32,
    )
    return result.reshape(9, act.shape[1], grad.shape[1])


def local(
    latents,
    time_embed,
    text_states,
    item_prompt,
    prompt_length,
    out_grad,
    resnorm_gain_a,
    resnorm_bias_a,
    conv_weight_a,
    conv_bias_a,
    time_weight,
    time_bias,
    resnorm_gain_b,
    resnorm_bias_b,
    conv_weight_b,
    conv_bias_b,
    attn_norm_gain,
    attn_norm_bias,
    qkv_weight,
    attn_out_weight,
    attn_out_bias,
    cross_norm_gain,
    cross_norm_bias,
    cross_query_weight,
    cross_kv_weight,
    cross_out_weight,
    cross_out_bias,
    geglu_norm_gain,
    geglu_norm_bias,
    geglu_in_weight,
    geglu_in_bias,
    geglu_out_weight,
    geglu_out_bias,
):
    row_count, local_chans = latents.shape
    half_chans = local_chans // 2
    own_rows = row_count // 4
    pair_rows = 2 * row_count
    offset = PIXELS // 4
    near_rows = row_count % PIXELS
    pair_items = pair_rows // PIXELS
    g_count = lax.axis_size("g")
    g_index, h_index = lax.axis_index("g"), lax.axis_index("h")
    place = 2 * lax.axis_index("x") + lax.axis_index("c")
    dp_index = 2 * g_index + h_index
    item_total = time_embed.shape[0]
    first_item = g_index * pair_items
    group_width = C // GROUPS
    channel = jnp.arange(half_chans) // group_width
    same_group = (channel[:, None] == channel[None, :]).astype(jnp.float32)

    def half_of(vector):
        return lax.dynamic_slice_in_dim(vector, h_index * half_chans, half_chans, axis=0)

    def group_means(first_term, second_term):
        sums = jnp.stack([first_term, second_term]).reshape(2, pair_items, PIXELS, half_chans)
        sums = jnp.einsum("sic,cd->sid", sums.sum(axis=2), same_group, precision=HIGH)
        return sums[:, :, None, :] / (PIXELS * group_width)

    def by_item(array_in):
        return array_in.reshape(pair_items, PIXELS, half_chans)

    def group_forward(array_in):
        means = group_means(array_in, array_in * array_in)
        inverse = lax.rsqrt(means[1] - means[0] * means[0] + EPS)
        return ((by_item(array_in) - means[0]) * inverse).reshape(array_in.shape), inverse

    def group_backward(grad_in, normed, inverse, gain):
        scaled = grad_in * gain
        means = group_means(scaled, scaled * normed)
        result = inverse * (by_item(scaled) - means[0] - by_item(normed) * means[1])
        return result.reshape(grad_in.shape)

    def layer_forward(array_in):
        mean = jnp.mean(array_in, axis=1, keepdims=True)
        square = jnp.mean(array_in * array_in, axis=1, keepdims=True)
        inverse = lax.rsqrt(square - mean * mean + EPS)
        return ((array_in - mean) * inverse, inverse)

    def layer_backward(grad_in, normed, inverse, gain):
        scaled = grad_in * gain
        first = jnp.mean(scaled, axis=1, keepdims=True)
        second = jnp.mean(scaled * normed, axis=1, keepdims=True)
        return inverse * (scaled - first - normed * second)

    def full_chans(array_in):
        return jnp.concatenate(gather_mp(array_in), axis=1)

    def full_rows(array_in):
        return jnp.concatenate(gather_mp(array_in), axis=0)

    def collect_rows(array_in):
        return scatter_sum_mp(narrow(array_in).reshape(2, 2, own_rows, array_in.shape[1]))

    def collect_chans(array_in):
        rows, chans = array_in.shape
        split = narrow(array_in).reshape(rows, 4, chans // 4).transpose(1, 0, 2)
        return scatter_sum_mp(split.reshape(2, 2, rows, chans // 4))

    def pair_to_half(array_in):
        split = array_in.reshape(pair_rows, 2, half_chans)
        sent = narrow(pick(split, 1 - h_index, 1))
        return pick(split, h_index, 1) + wide(swap(sent, "h"))

    def half_to_rows(array_in, rows_type):
        split = array_in.reshape(2, row_count, half_chans)
        kept = pick(split, h_index, 0)
        got = swap(pick(split, 1 - h_index, 0).astype(rows_type), "h").astype(array_in.dtype)
        first = h_index == 0
        return jnp.concatenate([jnp.where(first, kept, got), jnp.where(first, got, kept)], axis=1)

    def rows_to_half(array_in):
        split = array_in.reshape(row_count, 2, half_chans)
        kept = pick(split, h_index, 1)
        got = swap(pick(split, 1 - h_index, 1), "h")
        first = h_index == 0
        return jnp.concatenate([jnp.where(first, kept, got), jnp.where(first, got, kept)], axis=0)

    conv_a_full = lax.all_gather(conv_weight_a, "g", axis=1, tiled=True)
    conv_b_full = lax.all_gather(conv_weight_b, "g", axis=1, tiled=True)
    square_held = jnp.concatenate(
        [
            qkv_weight,
            cross_query_weight[None],
            attn_out_weight.T[None],
            cross_out_weight.T[None],
        ],
        axis=0,
    )
    square_near = lax.all_gather(square_held, "g", axis=1, tiled=True)
    square_full = gather_h(square_near.reshape(6, g_count, -1, local_chans), 2)
    square_full = square_full.reshape(6, C, local_chans)
    qkv_full, cross_query_full = square_full[:3], square_full[3]
    attn_out_full, cross_out_full = square_full[4], square_full[5]

    def to_units(array_in):
        split = array_in.reshape(*array_in.shape[:2], 2, -1)
        kept = pick(split, h_index, 2)
        got = swap(pick(split, 1 - h_index, 2), "h")
        first = h_index == 0
        return jnp.concatenate(
            [jnp.where(first, kept, got), jnp.where(first, got, kept)], axis=0
        )

    def from_units(array_in):
        split = array_in.reshape(2, -1, *array_in.shape[1:])
        kept = pick(split, h_index, 0)
        got = swap(pick(split, 1 - h_index, 0), "h")
        first = h_index == 0
        return jnp.concatenate(
            [jnp.where(first, kept, got), jnp.where(first, got, kept)], axis=2
        )

    geglu_in_full = lax.all_gather(to_units(geglu_in_weight), "g", axis=0, tiled=True)
    geglu_out_full = lax.all_gather(
        to_units(geglu_out_weight.T[:, None, :])[:, 0], "g", axis=0, tiled=True
    )
    half_units = geglu_in_weight.shape[2] // 2
    unit_bias = lax.dynamic_slice_in_dim(geglu_in_bias, h_index * half_units, half_units, axis=1)
    vectors = full_chans(
        jnp.stack(
            [
                attn_norm_gain,
                attn_norm_bias,
                attn_out_bias,
                cross_norm_gain,
                cross_norm_bias,
                cross_out_bias,
                geglu_norm_gain,
                geglu_norm_bias,
            ]
        )
    )
    attn_gain, attn_bias, attn_shift, cross_gain, cross_bias, cross_shift, geglu_gain, geglu_bias = vectors

    latents_even = shift_rows(latents, True, offset)
    latents_turned = wide(turn(latents_even, near_rows, True))
    latent_in = wide(rows_to_half(latents_even))
    time_in = narrow(jax.nn.silu(wide(time_embed)))
    temb_local = time_weight.shape[0]
    time_slice = lax.dynamic_slice_in_dim(time_in, dp_index * temb_local, temb_local, axis=1)
    time_part = sum_g(product(time_slice, time_weight))
    time_part = lax.dynamic_slice_in_dim(time_part, first_item, pair_items, axis=0)
    gain_a, gain_b = half_of(resnorm_gain_a), half_of(resnorm_gain_b)
    normed_a, inverse_a = group_forward(latent_in)
    pre_a = normed_a * gain_a + half_of(resnorm_bias_a)
    act_a = full_chans(narrow(jax.nn.silu(pre_a)))
    middle_part = conv_apply(act_a, conv_a_full).reshape(pair_items, PIXELS, local_chans)
    middle_part = (middle_part + time_part[:, None, :]).reshape(pair_rows, local_chans)
    middle = pair_to_half(middle_part) + half_of(conv_bias_a + time_bias)
    normed_b, inverse_b = group_forward(middle)
    pre_b = normed_b * gain_b + half_of(resnorm_bias_b)
    act_b = full_chans(narrow(jax.nn.silu(pre_b)))
    resid_part = conv_apply(act_b, conv_b_full).reshape(2, row_count, local_chans)
    resid_sent = swap(narrow(pick(resid_part, 1 - h_index, 0)), "h")
    resid_part = pick(resid_part, h_index, 0) + wide(resid_sent)
    resid = latents_turned + turn(resid_part, near_rows, True) + conv_bias_b

    resid_full = full_chans(narrow(resid))
    normed_full, _ = layer_forward(wide(resid_full))
    full_one = narrow(normed_full * attn_gain + attn_bias)
    resid_one = wide(lax.dynamic_slice_in_dim(resid_full, place * own_rows, own_rows, axis=0))
    normed_one, inverse_one = layer_forward(resid_one)
    qkv_rows = narrow(
        jnp.einsum("rc,kcd->krd", full_one, qkv_full, preferred_element_type=jnp.float32)
    )
    far_rows = swap(qkv_rows[1:, row_count - near_rows :], "h")
    heads_flops = 4 * row_count * PIXELS * local_chans
    attended = kernel_call(
        self_kernel,
        [in_vmem(), in_vmem()],
        [((row_count, local_chans), jnp.bfloat16)],
        heads_flops,
        qkv_rows,
        far_rows,
    )
    resid_two = resid_one + collect_rows(outer_cols(attended, attn_out_full)) + attn_shift
    normed_two, inverse_two = layer_forward(resid_two)
    full_two = full_rows(narrow(normed_two * cross_gain + cross_bias))
    cross_query = narrow(product(full_two, cross_query_full))
    text_rows = jnp.pad(text_states, ((0, 0), (0, TXT_PAD - TXT_LEN), (0, 0)))
    text_rows = text_rows.reshape(PROMPTS * TXT_PAD, TXT)
    text_local = cross_kv_weight.shape[1]
    text_slice = lax.dynamic_slice_in_dim(text_rows, dp_index * text_local, text_local, axis=1)
    text_part = jnp.einsum(
        "pt,ktd->kpd", text_slice, cross_kv_weight, preferred_element_type=jnp.float32
    )
    text_kv = sum_pixels(text_part)
    text_kv = text_kv.reshape(2, PROMPTS, TXT_PAD, local_chans)
    slots = jnp.where(h_index == 0, 0, (row_count + PIXELS - 1) // PIXELS)
    slots = slots + jnp.arange(row_count // PIXELS + 1, dtype=jnp.int32)
    slots = jnp.where(jnp.arange(slots.shape[0]) == slots.shape[0] - 1, row_count // PIXELS, slots)
    slot_prompt = jnp.take(item_prompt, first_item + slots)
    slot_length = jnp.take(prompt_length, slot_prompt)
    cross_flops = 4 * row_count * TXT_PAD * local_chans
    cross_attended = kernel_call(
        cross_kernel,
        [in_smem(), in_smem(), in_vmem(), in_vmem()],
        [((row_count, local_chans), jnp.bfloat16)],
        cross_flops,
        slot_prompt,
        slot_length,
        cross_query,
        text_kv,
    )
    resid_three = resid_two + collect_rows(outer_cols(cross_attended, cross_out_full)) + cross_shift
    normed_three, inverse_three = layer_forward(resid_three)
    full_three = jnp.concatenate(
        gather_eight(narrow(normed_three * geglu_gain + geglu_bias)), axis=0
    )
    pre_ff = (
        jnp.einsum("rc,cjf->rjf", full_three, geglu_in_full, preferred_element_type=jnp.float32)
        + unit_bias
    )
    hidden = narrow(geglu(pre_ff[:, 0], pre_ff[:, 1]))
    row_place = jnp.arange(8)[:, None, None] == 4 * h_index + place
    block_part = product(hidden, geglu_out_full.T).reshape(8, own_rows, C)
    block_part = block_part + jnp.where(row_place, resid_three[None], 0.0)
    block_part = narrow(block_part).reshape(2, row_count, 4, local_chans).transpose(0, 2, 1, 3)
    block_part = block_part.reshape(2, 2, 2, row_count, local_chans)
    block_turned = narrow(scatter_sum_eight(block_part) + geglu_out_bias)
    block_out = shift_rows(turn(block_turned, near_rows, False), False, offset)

    geglu_out_bias_grad = jnp.sum(wide(out_grad), axis=0)
    grad_turned = turn(shift_rows(out_grad, True, offset), near_rows, True)
    grad_full = full_chans(join_h(grad_turned, 0))
    grad_three = wide(
        lax.dynamic_slice_in_dim(grad_full, (4 * h_index + place) * own_rows, own_rows, axis=0)
    )
    geglu_out_weight_part = narrow(inner_rows(grad_full, hidden))
    d_hidden = product(grad_full, geglu_out_full)
    _, geglu_pull = jax.vjp(geglu, pre_ff[:, 0], pre_ff[:, 1])
    d_value, d_gate = geglu_pull(d_hidden)
    d_pre = jnp.stack([d_value, d_gate], axis=1)
    geglu_in_bias_grad = jnp.sum(d_pre, axis=0)
    d_pre_low = narrow(d_pre)
    geglu_in_weight_part = narrow(
        jnp.einsum("rc,rjf->cjf", full_three, d_pre_low, preferred_element_type=jnp.float32)
    )
    d_norm_three = jnp.einsum(
        "rjf,cjf->rc", d_pre_low, geglu_in_full, preferred_element_type=jnp.float32
    )
    d_norm_three = scatter_sum_eight(narrow(d_norm_three).reshape(2, 2, 2, own_rows, C))
    geglu_norm_gain_grad = jnp.sum(d_norm_three * normed_three, axis=0)
    geglu_norm_bias_grad = jnp.sum(d_norm_three, axis=0)
    grad_two = grad_three + layer_backward(d_norm_three, normed_three, inverse_three, geglu_gain)
    cross_out_bias_grad = jnp.sum(grad_two, axis=0)
    cross_full = full_rows(narrow(grad_two))
    cross_out_weight_part = narrow(inner_rows(cross_full, cross_attended))
    d_cross = narrow(product(cross_full, cross_out_full))
    d_cross_query, text_grad_part = kernel_call(
        cross_back_kernel,
        [in_smem(), in_smem(), in_vmem(), in_vmem(), in_vmem()],
        [
            ((row_count, local_chans), jnp.bfloat16),
            ((2, PROMPTS, TXT_PAD, local_chans), jnp.float32),
        ],
        3 * cross_flops,
        slot_prompt,
        slot_length,
        cross_query,
        text_kv,
        d_cross,
    )
    cross_query_weight_part = narrow(inner_rows(full_two, d_cross_query))
    d_norm_two = collect_rows(outer_cols(d_cross_query, cross_query_full))
    cross_norm_gain_grad = jnp.sum(d_norm_two * normed_two, axis=0)
    cross_norm_bias_grad = jnp.sum(d_norm_two, axis=0)
    grad_one = grad_two + layer_backward(d_norm_two, normed_two, inverse_two, cross_gain)
    attn_out_bias_grad = jnp.sum(grad_one, axis=0)
    attn_full = full_rows(narrow(grad_one))
    attn_out_weight_part = narrow(inner_rows(attn_full, attended))
    d_attended = narrow(product(attn_full, attn_out_full))
    d_qkv, d_far = kernel_call(
        self_back_kernel,
        [in_vmem(), in_vmem(), in_vmem()],
        [
            ((3, row_count, local_chans), jnp.bfloat16),
            ((2, near_rows, local_chans), jnp.bfloat16),
        ],
        3 * heads_flops,
        qkv_rows,
        far_rows,
        d_attended,
    )
    d_near = wide(swap(d_far, "h")) + wide(d_qkv[1:, row_count - near_rows :])
    d_qkv = d_qkv.at[1:, row_count - near_rows :].set(narrow(d_near))
    qkv_weight_part = narrow(
        jnp.einsum("rc,krd->kcd", full_one, d_qkv, preferred_element_type=jnp.float32)
    )
    d_norm_one = collect_rows(
        jnp.einsum("krd,kcd->rc", d_qkv, qkv_full, preferred_element_type=jnp.float32)
    )
    attn_norm_gain_grad = jnp.sum(d_norm_one * normed_one, axis=0)
    attn_norm_bias_grad = jnp.sum(d_norm_one, axis=0)
    grad_zero = grad_one + layer_backward(d_norm_one, normed_one, inverse_one, attn_gain)

    zero_blocks = narrow(grad_zero).reshape(own_rows, 4, local_chans).transpose(1, 0, 2)
    zero_turned = jnp.concatenate(exchange_mp(zero_blocks), axis=0)
    zero_rows = turn(zero_turned, near_rows, False)
    conv_bias_b_grad = jnp.sum(wide(zero_rows), axis=0)
    zero_pair = join_h(zero_rows, 0)
    conv_weight_b_part = narrow(conv_back_weight(act_b, zero_pair))
    d_pre_b = silu_back(collect_chans(conv_back_input(zero_pair, conv_b_full)), pre_b)
    resnorm_gain_b_grad = jnp.sum(d_pre_b * normed_b, axis=0)
    resnorm_bias_b_grad = jnp.sum(d_pre_b, axis=0)
    d_middle = group_backward(d_pre_b, normed_b, inverse_b, gain_b)
    time_part_grad = by_item(d_middle).sum(axis=1)
    middle_pair = join_h(narrow(d_middle), 1)
    conv_weight_a_part = narrow(conv_back_weight(act_a, middle_pair))
    d_pre_a = silu_back(collect_chans(conv_back_input(middle_pair, conv_a_full)), pre_a)
    resnorm_gain_a_grad = jnp.sum(d_pre_a * normed_a, axis=0)
    resnorm_bias_a_grad = jnp.sum(d_pre_a, axis=0)
    d_latents = group_backward(d_pre_a, normed_a, inverse_a, gain_a)
    d_latents = wide(zero_rows) + half_to_rows(d_latents, jnp.bfloat16)
    latents_grad = shift_rows(d_latents, False, offset)

    row_vectors = jnp.stack(
        [
            attn_norm_gain_grad,
            attn_norm_bias_grad,
            attn_out_bias_grad,
            cross_norm_gain_grad,
            cross_norm_bias_grad,
            cross_out_bias_grad,
            geglu_norm_gain_grad,
            geglu_norm_bias_grad,
        ]
    )
    row_blocks = row_vectors.reshape(8, 4, local_chans).transpose(1, 0, 2)
    row_sums = scatter_sum_mp(narrow(row_blocks).reshape(2, 2, 8, local_chans))
    early = jnp.concatenate(
        [
            row_sums,
            geglu_out_bias_grad[None],
            conv_bias_b_grad[None],
        ],
        axis=0,
    )
    early = sum_g(early + swap(early, "h"))
    in_bias_grad = join_h(sum_g(geglu_in_bias_grad), 1)
    time_held = jnp.zeros((item_total, half_chans), jnp.float32)
    time_held = lax.dynamic_update_slice_in_dim(time_held, time_part_grad, first_item, axis=0)
    late = jnp.concatenate(
        [
            time_held,
            resnorm_gain_a_grad[None],
            resnorm_bias_a_grad[None],
            resnorm_gain_b_grad[None],
            resnorm_bias_b_grad[None],
        ],
        axis=0,
    )
    late = join_h(sum_g(late), 1)
    time_grad, norm_grads = late[:item_total], late[item_total:]
    time_bias_grad = jnp.sum(time_grad, axis=0)
    time_weight_grad = inner_rows(time_slice, narrow(time_grad))
    text_grad = sum_pixels(text_grad_part.reshape(2, PROMPTS * TXT_PAD, local_chans))
    cross_kv_weight_grad = jnp.stack(
        [inner_rows(text_slice, text_grad[0]), inner_rows(text_slice, text_grad[1])]
    )

    def to_owner(array_in, dim):
        return lax.psum_scatter(array_in, "g", scatter_dimension=dim, tiled=True)

    def pair_sum(parts):
        stacked = jnp.stack(parts).reshape(len(parts), g_count, 2, -1, local_chans)
        return narrow(scatter_sum_h(stacked, 2)).reshape(len(parts), -1, local_chans)

    geglu_out_weight_grad = from_units(to_owner(geglu_out_weight_part, 0)[:, None, :])
    geglu_out_weight_grad = wide(geglu_out_weight_grad)[:, 0].T
    geglu_in_weight_grad = wide(from_units(to_owner(geglu_in_weight_part, 0)))
    out_parts = pair_sum([cross_query_weight_part, cross_out_weight_part, attn_out_weight_part])
    out_grads = wide(to_owner(out_parts, 1))
    cross_query_weight_grad = out_grads[0]
    cross_out_weight_grad, attn_out_weight_grad = out_grads[1].T, out_grads[2].T
    qkv_weight_grad = wide(to_owner(pair_sum(list(qkv_weight_part)), 1))
    conv_weight_b_grad = wide(to_owner(conv_weight_b_part, 1))
    conv_weight_a_grad = wide(to_owner(conv_weight_a_part, 1))
    return (
        block_out,
        latents_grad,
        norm_grads[0],
        norm_grads[1],
        conv_weight_a_grad,
        time_bias_grad,
        time_weight_grad,
        time_bias_grad,
        norm_grads[2],
        norm_grads[3],
        conv_weight_b_grad,
        early[9],
        early[0],
        early[1],
        qkv_weight_grad,
        attn_out_weight_grad,
        early[2],
        early[3],
        early[4],
        cross_query_weight_grad,
        cross_kv_weight_grad,
        cross_out_weight_grad,
        early[5],
        early[6],
        early[7],
        geglu_in_weight_grad,
        in_bias_grad,
        geglu_out_weight_grad,
        early[8],
    )


DP, MP = ("g", "h"), ("x", "c")
EVERY = P()
ROWS = P(DP, MP)
VECTOR = P(MP)
STACK = P(None, DP, MP)
TURNED = P(MP, DP)
GATED = P(DP, None, MP)


def solution(mesh):
    dp_count, mp_count = mesh.shape["dp"], mesh.shape["mp"]
    split = Mesh(mesh.devices.reshape(dp_count // 2, 2, mp_count // 2, 2), ("g", "h", "x", "c"))
    return jax.shard_map(
        local,
        mesh=split,
        in_specs=(
            (ROWS, EVERY, EVERY, EVERY, EVERY, ROWS)
            + (VECTOR, VECTOR, STACK, VECTOR, ROWS, VECTOR, VECTOR, VECTOR, STACK, VECTOR)
            + (VECTOR, VECTOR, STACK, TURNED, VECTOR)
            + (VECTOR, VECTOR, ROWS, STACK, TURNED, VECTOR)
            + (VECTOR, VECTOR, GATED, P(None, MP), TURNED, VECTOR)
        ),
        out_specs=(
            (ROWS, ROWS, VECTOR, VECTOR, STACK, VECTOR, ROWS, VECTOR, VECTOR, VECTOR, STACK, VECTOR)
            + (VECTOR, VECTOR, STACK, TURNED, VECTOR)
            + (VECTOR, VECTOR, ROWS, STACK, TURNED, VECTOR)
            + (VECTOR, VECTOR, GATED, P(None, MP), TURNED, VECTOR)
        ),
        check_vma=False,
    )
```
